256 devices in a mesh: sta: 32 (over z_lo, x, core), tm: 8 (over z_hi, y).
Axes of the slice: x: 4, y: 4, z: 8 (z_hi: 2, z_lo: 4; z = z_hi * 4 + z_lo), core: 2. Of those that a mesh axis runs over, the one named last changes fastest.
Arguments:
- records: bfloat16 [64, 3, 4096], P('sta', None, 'tm'), may hold values from -6 to 6
- templates: bfloat16 [512, 64, 3, 150], P(None, 'sta'), may hold values from -6 to 6
- moveout: int32 [512, 64], P(None, 'sta'), may hold values from 0 to 256
- gap_start: int32 [64, 3], P('sta'), may hold values from 0 to 4095
- gap_length: int32 [64, 3], P('sta'), may hold values from 0 to 599
Outputs:
- detection: float32 [512, 4096], P('sta', 'tm')
The draws below stay inside these ranges and needn't reach their ends.
Inputs may be any that keep to these rules, and one draw needn't show every extreme that they name: `gap_length`: each channel has one gap, counted in samples of the whole window; it may run past the window's end.
All inputs are finite; a program needn't handle non-finite values.
Results may differ from the reference program's by a relative error of at most 0.0041.
Values may be sent and summed in bfloat16 or wider, within the bound.
A program may use at most 64 MiB of HBM per device.

```python
import math
import jax
import jax.numpy as jnp
from jax import lax

CHANNELS = 3
TEMPLATE_LEN = 150
TEMPLATES = 512
MAXMO = 256
STATIONS = 64
NT = 4096


def set_ends(entries, key, least, largest):
    place = [jax.random.randint(jax.random.fold_in(key, axis), (), 0, length) for axis, length in enumerate(entries.shape)]
    main_axis = entries.shape.index(max(entries.shape))
    next_to = place[:main_axis] + [(place[main_axis] + 1) % entries.shape[main_axis]] + place[main_axis + 1:]
    return entries.at[tuple(place)].set(least).at[tuple(next_to)].set(largest)


def level_of(key, extent, split, low, high):
    def one(position, shards_of):
        steps = jax.random.uniform(jax.random.fold_in(jax.random.fold_in(key, 6), position), (shards_of,), jnp.float32, low / len(split), high / len(split))
        return jnp.repeat(jnp.exp(steps), extent[position] // shards_of).reshape((-1,) + (1,) * (len(extent) - position - 1))

    gain = one(*split[0])
    for cut in split[1:]:
        gain = gain * one(*cut)
    return gain


def normal_values(rng, shape, scale, most, split=(), held_as=jnp.bfloat16):
    array = scale * jax.random.normal(rng, shape, jnp.float32)
    if split:
        array = array * level_of(rng, shape, split, -0.22, 0.18)
    return jnp.clip(array, -most, most).astype(held_as)


def setup_inputs(seed: int = 0) -> dict:
    keys = jax.random.split(jax.random.key(seed), 6)
    return {
        "records": normal_values(keys[0], (STATIONS, CHANNELS, NT), 1.0, 6.0, ((0, 32), (2, 8))),
        "templates": normal_values(keys[1], (TEMPLATES, STATIONS, CHANNELS, TEMPLATE_LEN), 1.0, 6.0, ((1, 32),)),
        "moveout": set_ends(jax.random.randint(keys[2], (TEMPLATES, STATIONS), 0, MAXMO + 1), jax.random.fold_in(keys[2], 1), 0, MAXMO).astype(jnp.int32),
        "gap_start": set_ends(jax.random.randint(keys[3], (STATIONS, CHANNELS), 0, NT), jax.random.fold_in(keys[3], 1), 0, NT - 1).astype(jnp.int32),
        "gap_length": set_ends(jax.random.randint(keys[4], (STATIONS, CHANNELS), 0, 4 * TEMPLATE_LEN), jax.random.fold_in(keys[4], 1), 0, (4 * TEMPLATE_LEN) - 1).astype(jnp.int32),
    }


def hankel(extended, full_width):
    return jnp.stack([extended[..., offset:offset + full_width] for offset in range(TEMPLATE_LEN)], axis=-2)

def whiten(extended, full_width):
    widened = hankel(extended, full_width).astype(jnp.float32)
    energy = lax.optimization_barrier(jnp.sum(widened * widened, axis=-2, keepdims=True))
    return (widened / jnp.sqrt(jnp.maximum(energy, 1.0))).astype(jnp.bfloat16)

def unit_templates(templates):
    widened = templates.astype(jnp.float32)
    return (widened / jnp.sqrt(lax.optimization_barrier(jnp.sum(widened * widened, axis=-1, keepdims=True)) + 1e-06)).astype(jnp.bfloat16)

def gap_mask(positions, gap_start, gap_length):
    first = gap_start[..., None]
    return (positions < first) | (positions >= first + gap_length[..., None])

def reference(records, templates, moveout, gap_start, gap_length):
    total_len = records.shape[-1]
    halo_width = MAXMO + TEMPLATE_LEN - 1
    extended = jnp.pad(records, ((0, 0), (0, 0), (0, halo_width)))
    positions = jnp.arange(total_len + halo_width, dtype=jnp.int32)
    kept_mask = gap_mask(positions, gap_start, gap_length)
    extended = jnp.where(kept_mask, extended, jnp.zeros_like(extended))
    full_width = total_len + MAXMO
    normed = unit_templates(templates)
    columns = jnp.arange(total_len, dtype=jnp.int32)

    def station_step(running, inputs):
        station_data, weights, lag_rows = inputs
        lagged = whiten(station_data, full_width).reshape(CHANNELS * TEMPLATE_LEN, full_width)
        weight_rows = weights.reshape(weights.shape[0], CHANNELS * TEMPLATE_LEN)
        correlation = jnp.dot(weight_rows, lagged, preferred_element_type=jnp.float32)
        shifted = jnp.take_along_axis(correlation, lag_rows[:, None] + columns[None, :], axis=1)
        return (running + shifted, None)
    initial = jnp.zeros((TEMPLATES, total_len), jnp.float32)
    stacked, _ = lax.scan(station_step, initial, (extended, jnp.swapaxes(normed, 0, 1), moveout.T))
    return stacked * math.sqrt(TEMPLATE_LEN / (3.0 * STATIONS))
```

```python
import functools
import math

import jax
import jax.numpy as jnp
from jax import lax
from jax.experimental import pallas as pl
from jax.experimental.pallas import tpu as pltpu
from jax.sharding import PartitionSpec as P

CHANNELS = 3
TEMPLATE_LEN = 150
TEMPLATES = 512
MAXMO = 256
NT = 4096
SLICE = 512
WIDE = 1024
FULL = SLICE + MAXMO
ROWS = 160
DEPTH = 512
MESH = pl.DeviceIdType.MESH


def kernel(
    scale,
    templates,
    records,
    moveout,
    gap_start,
    gap_length,
    out,
    packed,
    unit32,
    unit_t,
    own,
    halo,
    moves,
    series,
    rolled,
    inverse,
    hankel,
    corr,
    lag,
    half_send,
    half_recv,
    half_own,
    x_send,
    x_recv,
    x_own,
    z_send,
    z_recv,
    local_sem,
    halo_sem,
    half_sem,
    x_sem,
    z_sem,
):
    sta = lax.axis_index("sta")
    tm = lax.axis_index("tm")
    core = lax.rem(sta, 2)
    xx = lax.rem(sta // 2, 4)
    zz = sta // 8

    def at(z, x, c):
        return z * 8 + x * 2 + c

    sibling = at(zz, xx, 1 - core)
    x_peers = [at(zz, lax.rem(xx + d, 4), core) for d in range(1, 4)]
    z_peers = [at(lax.rem(zz + d, 4), xx, core) for d in range(1, 4)]

    barrier = pltpu.get_barrier_semaphore()
    pl.semaphore_signal(
        barrier, inc=1, device_id={"tm": lax.rem(tm + 1, 8)}, device_id_type=MESH
    )
    for peer in [sibling] + x_peers + z_peers:
        pl.semaphore_signal(barrier, inc=1, device_id={"sta": peer}, device_id_type=MESH)

    loads = [
        pltpu.make_async_copy(records, own, local_sem.at[0]),
        pltpu.make_async_copy(moveout, moves, local_sem.at[1]),
        pltpu.make_async_copy(templates, packed, local_sem.at[2]),
    ]
    for load in loads:
        load.start()

    pl.semaphore_wait(barrier, 8)
    halo_copy = pltpu.make_async_remote_copy(
        src_ref=records,
        dst_ref=halo,
        send_sem=halo_sem.at[0],
        recv_sem=halo_sem.at[1],
        device_id={"tm": lax.rem(tm + 7, 8)},
        device_id_type=MESH,
    )
    halo_copy.start()

    for load in loads:
        load.wait()

    for s in range(2):
        for q in range(4):
            line = moves[s : s + 1, 128 * q : 128 * (q + 1)]
            lag[s, 128 * q : 128 * (q + 1), :] = jnp.broadcast_to(line, (128, 128)).T

    unit32[3600:3680, :] = jnp.zeros((80, 128), jnp.float32)
    for c in range(CHANNELS):
        wide = packed[1200 * c : 1200 * (c + 1), :].astype(jnp.float32).reshape(150, 8, 128)
        norm = 1.0 / jnp.sqrt(jnp.sum(wide * wide, axis=0, keepdims=True) + 1e-06)
        unit32[1200 * c : 1200 * (c + 1), :] = (wide * norm).reshape(1200, 128)
    row = lax.broadcasted_iota(jnp.int32, (ROWS, 128), 0)
    for s in range(2):
        for q in range(4):
            parts = []
            for c in range(CHANNELS):
                taken = unit32[pl.ds(1200 * c + 2 * q + s, ROWS, stride=8), :]
                parts.append(jnp.where(row < TEMPLATE_LEN, taken, 0.0))
            parts.append(jnp.zeros((DEPTH - 3 * ROWS, 128), jnp.float32))
            block = jnp.concatenate(parts, axis=0).astype(jnp.bfloat16)
            unit_t[s, 128 * q : 128 * (q + 1), :] = block.T

    halo_copy.wait()

    series[...] = jnp.zeros_like(series)
    for c in range(CHANNELS):
        series[2 * c : 2 * c + 2, 0:SLICE] = own[c].astype(jnp.float32)
        series[2 * c : 2 * c + 2, SLICE:WIDE] = halo[c].astype(jnp.float32)
    line = lax.broadcasted_iota(jnp.int32, (8, WIDE), 0)
    position = lax.broadcasted_iota(jnp.int32, (8, WIDE), 1) + tm * SLICE
    first = jnp.zeros((8, WIDE), jnp.int32)
    length = jnp.zeros((8, WIDE), jnp.int32)
    for s in range(2):
        for c in range(CHANNELS):
            first = jnp.where(line == 2 * c + s, gap_start[s, c], first)
            length = jnp.where(line == 2 * c + s, gap_length[s, c], length)
    kept = ((position < first) | (position >= first + length)) & (position < NT)
    masked = jnp.where(kept, series[...], 0.0)

    def ahead(value, by):
        return pltpu.roll(value, WIDE - by, 1)

    for r in range(8):
        moved = masked if r == 0 else ahead(masked, r)
        for b in range(8):
            rolled[b, 8 * r : 8 * (r + 1), :] = moved[:, 128 * b : 128 * (b + 1)]
    sums = {1: masked * masked}
    for power in range(7):
        width = 1 << power
        sums[2 * width] = sums[width] + ahead(sums[width], width)
    energy = (sums[128] + ahead(sums[16], 128)) + (ahead(sums[4], 144) + ahead(sums[2], 148))
    inverse[...] = (1.0 / jnp.sqrt(jnp.maximum(energy, 1.0)))[:, :FULL]

    for s in range(2):
        hankel[s, 3 * ROWS : DEPTH, :] = jnp.zeros((DEPTH - 3 * ROWS, FULL), jnp.bfloat16)
        for c in range(CHANNELS):
            eight = jnp.concatenate(
                [rolled[b, pl.ds(2 * c + s, 8, stride=8), :] for b in range(8)], axis=1
            )
            weight = inverse[2 * c + s : 2 * c + s + 1, :]
            for a in range(ROWS // 16):
                top = eight if a == 0 else ahead(eight, 16 * a)
                low = ahead(eight, 16 * a + 8)
                both = jnp.concatenate([top[:, :FULL] * weight, low[:, :FULL] * weight], axis=0)
                hankel[s, ROWS * c + 16 * a : ROWS * c + 16 * (a + 1), :] = both.astype(
                    jnp.bfloat16
                )

    lane = lax.broadcasted_iota(jnp.int32, (16, 128), 1)

    def correlate(side, store):
        for s in range(2):
            rows = [
                unit_t[s, pl.ds(pl.multiple_of(32 * g + 16 * side, 16), 16), :] for g in range(16)
            ]
            corr[s] = jnp.dot(
                jnp.concatenate(rows, axis=0), hankel[s], preferred_element_type=jnp.float32
            )

        def group(g, carry):
            base = pl.multiple_of(16 * g, 16)
            start = pl.multiple_of(32 * g + 16 * side, 16)
            total = [None] * 4
            for s in range(2):
                move = lag[s, pl.ds(start, 16), :]
                near = move <= lane
                middle = move <= lane + 128
                index = (lane + move) & 127
                pieces = [corr[s, pl.ds(base, 16), 128 * j : 128 * (j + 1)] for j in range(6)]
                for j in range(4):
                    mixed = jnp.where(
                        near, pieces[j], jnp.where(middle, pieces[j + 1], pieces[j + 2])
                    )
                    moved = jnp.take_along_axis(mixed, index, axis=1, mode="promise_in_bounds")
                    total[j] = moved if s == 0 else total[j] + moved
            store(g, jnp.concatenate(total, axis=1))
            return carry

        lax.fori_loop(0, 16, group, 0)

    def to_send(g, value):
        half_send[g // 4, lax.rem(g, 4)] = value.astype(jnp.bfloat16)

    def to_own(g, value):
        half_own[g // 4, lax.rem(g, 4)] = value

    correlate(1 - core, to_send)
    half_copy = pltpu.make_async_remote_copy(
        src_ref=half_send,
        dst_ref=half_recv,
        send_sem=half_sem.at[0],
        recv_sem=half_sem.at[1],
        device_id={"sta": sibling},
        device_id_type=MESH,
    )
    half_copy.start()
    correlate(core, to_own)
    half_copy.wait()

    x_copies = []
    for d in (2, 1, 3):
        target = lax.rem(xx + d, 4)
        x_send[d - 1] = (
            half_own[:, target] + half_recv[:, target].astype(jnp.float32)
        ).astype(jnp.bfloat16)
        copy = pltpu.make_async_remote_copy(
            src_ref=x_send.at[d - 1],
            dst_ref=x_recv.at[d - 1],
            send_sem=x_sem.at[0, d - 1],
            recv_sem=x_sem.at[1, d - 1],
            device_id={"sta": x_peers[d - 1]},
            device_id_type=MESH,
        )
        copy.start()
        x_copies.append(copy)
    x_own[...] = half_own[:, xx] + half_recv[:, xx].astype(jnp.float32)
    for copy in x_copies:
        copy.wait()

    def over_x(z):
        total = x_own[z]
        for d in range(3):
            total = total + x_recv[d, z].astype(jnp.float32)
        return total

    z_copies = []
    for d in (2, 1, 3):
        z_send[d - 1] = over_x(lax.rem(zz + d, 4)).astype(jnp.bfloat16)
        copy = pltpu.make_async_remote_copy(
            src_ref=z_send.at[d - 1],
            dst_ref=z_recv.at[d - 1],
            send_sem=z_sem.at[0, d - 1],
            recv_sem=z_sem.at[1, d - 1],
            device_id={"sta": z_peers[d - 1]},
            device_id_type=MESH,
        )
        copy.start()
        z_copies.append(copy)
    total = over_x(zz)
    for copy in z_copies:
        copy.wait()
    for d in range(3):
        total = total + z_recv[d].astype(jnp.float32)
    out[...] = total * scale


def shards(records, templates, moveout, gap_start, gap_length):
    stations = records.shape[0] * lax.axis_size("sta")
    scale = math.sqrt(TEMPLATE_LEN / (3.0 * stations))
    lines = jnp.transpose(templates, (2, 3, 1, 0)).reshape(450, 2, 4, 128)
    lines = jnp.transpose(lines, (0, 2, 1, 3)).reshape(3600, 128)
    whole = pl.BlockSpec(memory_space=pl.ANY)
    scalars = pl.BlockSpec(memory_space=pltpu.SMEM)
    return pl.pallas_call(
        functools.partial(kernel, scale),
        out_shape=jax.ShapeDtypeStruct((16, SLICE), jnp.float32),
        in_specs=[whole, whole, whole, scalars, scalars],
        out_specs=pl.BlockSpec(memory_space=pltpu.VMEM),
        scratch_shapes=[
            pltpu.VMEM((3600, 128), jnp.bfloat16),
            pltpu.VMEM((3680, 128), jnp.float32),
            pltpu.VMEM((2, TEMPLATES, DEPTH), jnp.bfloat16),
            pltpu.VMEM((3, 2, SLICE), jnp.bfloat16),
            pltpu.VMEM((3, 2, SLICE), jnp.bfloat16),
            pltpu.VMEM((2, TEMPLATES), jnp.int32),
            pltpu.VMEM((8, WIDE), jnp.float32),
            pltpu.VMEM((8, 64, 128), jnp.float32),
            pltpu.VMEM((8, FULL), jnp.float32),
            pltpu.VMEM((2, DEPTH, FULL), jnp.bfloat16),
            pltpu.VMEM((2, 256, FULL), jnp.float32),
            pltpu.VMEM((2, TEMPLATES, 128), jnp.int32),
            pltpu.VMEM((4, 4, 16, SLICE), jnp.bfloat16),
            pltpu.VMEM((4, 4, 16, SLICE), jnp.bfloat16),
            pltpu.VMEM((4, 4, 16, SLICE), jnp.float32),
            pltpu.VMEM((3, 4, 16, SLICE), jnp.bfloat16),
            pltpu.VMEM((3, 4, 16, SLICE), jnp.bfloat16),
            pltpu.VMEM((4, 16, SLICE), jnp.float32),
            pltpu.VMEM((3, 16, SLICE), jnp.bfloat16),
            pltpu.VMEM((3, 16, SLICE), jnp.bfloat16),
            pltpu.SemaphoreType.DMA((3,)),
            pltpu.SemaphoreType.DMA((2,)),
            pltpu.SemaphoreType.DMA((2,)),
            pltpu.SemaphoreType.DMA((2, 3)),
            pltpu.SemaphoreType.DMA((2, 3)),
        ],
        compiler_params=pltpu.CompilerParams(
            collective_id=0, has_side_effects=True, vmem_limit_bytes=40 * 1024 * 1024
        ),
    )(lines, jnp.transpose(records, (1, 0, 2)), jnp.transpose(moveout, (1, 0)), gap_start, gap_length)


def solution(mesh):
    placed = (
        P("sta", None, "tm"),
        P(None, "sta", None, None),
        P(None, "sta"),
        P("sta", None),
        P("sta", None),
    )
    return jax.shard_map(
        shards, mesh=mesh, in_specs=placed, out_specs=P("sta", "tm"), check_vma=False
    )
```

```python
import functools
import math

import jax
import jax.numpy as jnp
from jax import lax
from jax.experimental import pallas as pl
from jax.experimental.pallas import tpu as pltpu
from jax.sharding import PartitionSpec as P

CHANNELS = 3
TEMPLATE_LEN = 150
TEMPLATES = 512
MAXMO = 256
NT = 4096
SLICE = 512
WIDE = 1024
FULL = SLICE + MAXMO
NEAR = 256
ROWS = 160
DEPTH = 512
MESH = pl.DeviceIdType.MESH


def paired(index, by):
    return (index, index + 1 - 2 * lax.rem(index, 2), lax.rem(index + 2, 4), 3 - index)[by]


def kernel(
    scale,
    templates,
    records,
    moveout,
    gap_start,
    gap_length,
    out,
    packed,
    unit32,
    unit_t,
    own,
    halo,
    moves,
    gaps,
    series,
    rolled,
    inverse,
    hankel,
    corr,
    lag,
    half_send,
    half_recv,
    half_own,
    part_send,
    part_recv,
    part_own,
    local_sem,
    halo_sem,
    half_sem,
    send_sem,
    recv_sem,
):
    sta = lax.axis_index("sta")
    tm = lax.axis_index("tm")
    core = lax.rem(sta, 2)
    xx = lax.rem(sta // 2, 4)
    zz = sta // 8
    zs = [paired(zz, a) for a in range(4)]
    xs = [paired(xx, b) for b in range(4)]

    def at(a, b, c):
        return {"sta": zs[a] * 8 + xs[b] * 2 + c}

    sibling = at(0, 0, 1 - core)
    barrier = pltpu.get_barrier_semaphore()

    @pl.when(tm < 7)
    def _():
        pl.semaphore_signal(
            barrier, inc=1, device_id={"tm": lax.rem(tm + 1, 8)}, device_id_type=MESH
        )

    for a in (3, 2, 1, 0):
        for b in (2, 1, 3, 0):
            if (a, b) != (0, 0):
                pl.semaphore_signal(barrier, inc=1, device_id=at(a, b, core), device_id_type=MESH)
    pl.semaphore_signal(barrier, inc=1, device_id=sibling, device_id_type=MESH)

    loads = [
        pltpu.make_async_copy(records, own, local_sem.at[0]),
        pltpu.make_async_copy(gap_start, gaps.at[0], local_sem.at[1]),
        pltpu.make_async_copy(gap_length, gaps.at[1], local_sem.at[2]),
        pltpu.make_async_copy(moveout, moves, local_sem.at[3]),
        pltpu.make_async_copy(templates, packed, local_sem.at[4]),
    ]
    for load in loads:
        load.start()

    @pl.when(tm == 7)
    def _():
        halo[...] = jnp.zeros_like(halo)

    for load in loads[:4]:
        load.wait()

    for s in range(2):
        for q in range(4):
            line = moves[s : s + 1, 128 * q : 128 * (q + 1)]
            lag[s, 128 * q : 128 * (q + 1), :] = jnp.broadcast_to(line, (128, 128)).T

    pl.semaphore_wait(barrier, 16 + jnp.where(tm > 0, 1, 0))
    halo_copy = pltpu.make_async_remote_copy(
        src_ref=own,
        dst_ref=halo,
        send_sem=halo_sem.at[0],
        recv_sem=halo_sem.at[1],
        device_id={"tm": lax.rem(tm + 7, 8)},
        device_id_type=MESH,
    )

    @pl.when(tm > 0)
    def _():
        halo_copy.start()

    loads[4].wait()

    unit32[3600:3680, :] = jnp.zeros((80, 128), jnp.float32)
    for c in range(CHANNELS):
        wide = packed[1200 * c : 1200 * (c + 1), :].astype(jnp.float32).reshape(150, 8, 128)
        norm = 1.0 / jnp.sqrt(jnp.sum(wide * wide, axis=0, keepdims=True) + 1e-06)
        unit32[1200 * c : 1200 * (c + 1), :] = (wide * norm).reshape(1200, 128)
    row = lax.broadcasted_iota(jnp.int32, (ROWS, 128), 0)
    for s in range(2):
        for q in range(4):
            parts = []
            for c in range(CHANNELS):
                taken = unit32[pl.ds(1200 * c + 2 * q + s, ROWS, stride=8), :]
                parts.append(jnp.where(row < TEMPLATE_LEN, taken, 0.0))
            parts.append(jnp.zeros((DEPTH - 3 * ROWS, 128), jnp.float32))
            block = jnp.concatenate(parts, axis=0).astype(jnp.bfloat16)
            unit_t[s, 128 * q : 128 * (q + 1), :] = block.T

    series[...] = jnp.zeros_like(series)
    for c in range(CHANNELS):
        series[2 * c : 2 * c + 2, 0:SLICE] = own[c].astype(jnp.float32)

    def spread(begin, end, base, stop):
        span = stop - base
        width = end - begin
        skip = begin - base
        line = lax.broadcasted_iota(jnp.int32, (8, span), 0)
        position = lax.broadcasted_iota(jnp.int32, (8, span), 1) + (tm * SLICE + base)
        first = jnp.zeros((8, span), jnp.int32)
        length = jnp.zeros((8, span), jnp.int32)
        for s in range(2):
            for c in range(CHANNELS):
                first = jnp.where(line == 2 * c + s, gaps[0, s, c], first)
                length = jnp.where(line == 2 * c + s, gaps[1, s, c], length)
        kept = ((position < first) | (position >= first + length)) & (position < NT)
        masked = jnp.where(kept, series[:, base:stop], 0.0)

        def ahead(value, by):
            return pltpu.roll(value, span - by, 1) if by else value

        for r in range(8):
            moved = ahead(masked, r)
            for b in range(span // 128):
                rolled[b, 8 * r : 8 * (r + 1), :] = moved[:, 128 * b : 128 * (b + 1)]
        sums = {1: masked * masked}
        for power in range(7):
            step = 1 << power
            sums[2 * step] = sums[step] + ahead(sums[step], step)
        energy = (sums[128] + ahead(sums[16], 128)) + (ahead(sums[4], 144) + ahead(sums[2], 148))
        inverse[:, begin:end] = (1.0 / jnp.sqrt(jnp.maximum(energy, 1.0)))[:, skip : skip + width]
        for s in range(2):
            hankel[s, 3 * ROWS : DEPTH, begin:end] = jnp.zeros(
                (DEPTH - 3 * ROWS, width), jnp.bfloat16
            )
            for c in range(CHANNELS):
                eight = jnp.concatenate(
                    [rolled[b, pl.ds(2 * c + s, 8, stride=8), :] for b in range(span // 128)],
                    axis=1,
                )
                weight = inverse[2 * c + s : 2 * c + s + 1, begin:end]
                for g in range(ROWS // 16):
                    pair = [
                        ahead(eight, 16 * g + 8 * h)[:, skip : skip + width] * weight
                        for h in range(2)
                    ]
                    hankel[s, ROWS * c + 16 * g : ROWS * c + 16 * (g + 1), begin:end] = (
                        jnp.concatenate(pair, axis=0).astype(jnp.bfloat16)
                    )

    def blocks(chunk):
        return [(a, b) for a in ((3, 2), (1, 0))[chunk] for b in (2, 1, 3, 0)]

    def first_row(a, b, side):
        return pl.multiple_of(128 * zs[a] + 32 * xs[b] + 16 * side, 16)

    def multiply(chunk, slot, side, begin, end):
        for s in range(2):
            rows = [unit_t[s, pl.ds(first_row(a, b, side), 16), :] for a, b in blocks(chunk)]
            corr[s, 128 * slot : 128 * (slot + 1), begin:end] = jnp.dot(
                jnp.concatenate(rows, axis=0),
                hankel[s, :, begin:end],
                preferred_element_type=jnp.float32,
            )

    lane = lax.broadcasted_iota(jnp.int32, (16, 128), 1)

    def shift(chunk, slot, side, store):
        for g, (a, b) in enumerate(blocks(chunk)):
            base = 128 * slot + 16 * g
            total = [None] * 4
            for s in range(2):
                move = lag[s, pl.ds(first_row(a, b, side), 16), :]
                near = move <= lane
                middle = move <= lane + 128
                index = (lane + move) & 127
                pieces = [corr[s, base : base + 16, 128 * j : 128 * (j + 1)] for j in range(6)]
                for j in range(4):
                    mixed = jnp.where(
                        near, pieces[j], jnp.where(middle, pieces[j + 1], pieces[j + 2])
                    )
                    moved = jnp.take_along_axis(mixed, index, axis=1, mode="promise_in_bounds")
                    total[j] = moved if s == 0 else total[j] + moved
            store(8 * chunk + g, jnp.concatenate(total, axis=1))

    def to_send(place, value):
        half_send[place] = value.astype(jnp.bfloat16)

    def to_own(place, value):
        half_own[place] = value

    def half_copy(chunk):
        return pltpu.make_async_remote_copy(
            src_ref=half_send.at[pl.ds(8 * chunk, 8)],
            dst_ref=half_recv.at[pl.ds(8 * chunk, 8)],
            send_sem=half_sem.at[0, chunk],
            recv_sem=half_sem.at[1, chunk],
            device_id=sibling,
            device_id_type=MESH,
        )

    def part_copy(a, b):
        place = 4 * a + b
        return pltpu.make_async_remote_copy(
            src_ref=part_send.at[place],
            dst_ref=part_recv.at[place],
            send_sem=send_sem.at[place],
            recv_sem=recv_sem.at[place],
            device_id=at(a, b, core),
            device_id_type=MESH,
        )

    stages = [(0, 0, 1 - core), (1, 1, 1 - core), (0, 2, core), (1, 3, core)]
    spread(0, NEAR, 0, SLICE)
    for chunk, slot, side in stages:
        multiply(chunk, slot, side, 0, NEAR)

    @pl.when(tm > 0)
    def _():
        halo_copy.wait_send()

    @pl.when(tm < 7)
    def _():
        halo_copy.wait_recv()

    for c in range(CHANNELS):
        series[2 * c : 2 * c + 2, SLICE:WIDE] = halo[c].astype(jnp.float32)
    spread(NEAR, FULL, NEAR, WIDE)

    copies = []
    for chunk, slot, side in stages:
        multiply(chunk, slot, side, NEAR, FULL)
        shift(chunk, slot, side, to_send if slot < 2 else to_own)
        copy = half_copy(chunk)
        if slot < 2:
            copy.start()
            continue
        copy.wait()
        for g, (a, b) in enumerate(blocks(chunk)):
            place = 8 * chunk + g
            value = half_own[place] + half_recv[place].astype(jnp.float32)
            if (a, b) == (0, 0):
                part_own[...] = value
            else:
                part_send[4 * a + b] = value.astype(jnp.bfloat16)
                part = part_copy(a, b)
                part.start()
                copies.append((4 * a + b, part))

    total = part_own[...]
    for place, part in copies:
        part.wait()
        total = total + part_recv[place].astype(jnp.float32)
    out[...] = total * scale


def shards(records, templates, moveout, gap_start, gap_length):
    stations = records.shape[0] * lax.axis_size("sta")
    scale = math.sqrt(TEMPLATE_LEN / (3.0 * stations))
    lines = jnp.transpose(templates, (2, 3, 1, 0)).reshape(450, 2, 4, 128)
    lines = jnp.transpose(lines, (0, 2, 1, 3)).reshape(3600, 128)
    whole = pl.BlockSpec(memory_space=pltpu.HBM)
    return pl.pallas_call(
        functools.partial(kernel, scale),
        out_shape=jax.ShapeDtypeStruct((16, SLICE), jnp.float32),
        in_specs=[whole] * 5,
        out_specs=pl.BlockSpec(memory_space=pltpu.VMEM),
        scratch_shapes=[
            pltpu.VMEM((3600, 128), jnp.bfloat16),
            pltpu.VMEM((3680, 128), jnp.float32),
            pltpu.VMEM((2, TEMPLATES, DEPTH), jnp.bfloat16),
            pltpu.VMEM((3, 2, SLICE), jnp.bfloat16),
            pltpu.VMEM((3, 2, SLICE), jnp.bfloat16),
            pltpu.VMEM((2, TEMPLATES), jnp.int32),
            pltpu.SMEM((2, 2, 3), jnp.int32),
            pltpu.VMEM((8, WIDE), jnp.float32),
            pltpu.VMEM((8, 64, 128), jnp.float32),
            pltpu.VMEM((8, FULL), jnp.float32),
            pltpu.VMEM((2, DEPTH, FULL), jnp.bfloat16),
            pltpu.VMEM((2, TEMPLATES, FULL), jnp.float32),
            pltpu.VMEM((2, TEMPLATES, 128), jnp.int32),
            pltpu.VMEM((16, 16, SLICE), jnp.bfloat16),
            pltpu.VMEM((16, 16, SLICE), jnp.bfloat16),
            pltpu.VMEM((16, 16, SLICE), jnp.float32),
            pltpu.VMEM((16, 16, SLICE), jnp.bfloat16),
            pltpu.VMEM((16, 16, SLICE), jnp.bfloat16),
            pltpu.VMEM((16, SLICE), jnp.float32),
            pltpu.SemaphoreType.DMA((5,)),
            pltpu.SemaphoreType.DMA((2,)),
            pltpu.SemaphoreType.DMA((2, 2)),
            pltpu.SemaphoreType.DMA((16,)),
            pltpu.SemaphoreType.DMA((16,)),
        ],
        compiler_params=pltpu.CompilerParams(
            collective_id=0, has_side_effects=True, vmem_limit_bytes=40 * 1024 * 1024
        ),
    )(
        *[
            pltpu.with_memory_space_constraint(value, pltpu.HBM)
            for value in (
                lines,
                jnp.transpose(records, (1, 0, 2)),
                jnp.transpose(moveout, (1, 0)),
                gap_start,
                gap_length,
            )
        ]
    )


def solution(mesh):
    placed = (
        P("sta", None, "tm"),
        P(None, "sta", None, None),
        P(None, "sta"),
        P("sta", None),
        P("sta", None),
    )
    return jax.shard_map(
        shards, mesh=mesh, in_specs=placed, out_specs=P("sta", "tm"), check_vma=False
    )
```

```python
import functools
import math

import jax
import jax.numpy as jnp
from jax import lax
from jax.experimental import pallas as pl
from jax.experimental.pallas import tpu as pltpu
from jax.sharding import PartitionSpec as P

CHANNELS = 3
TEMPLATE_LEN = 150
TEMPLATES = 512
MAXMO = 256
NT = 4096
SLICE = 512
WIDE = 1024
FULL = SLICE + MAXMO
NEAR = 256
ROWS = 160
DEPTH = 512
MESH = pl.DeviceIdType.MESH


def paired(index, by):
    return (index, index + 1 - 2 * lax.rem(index, 2), lax.rem(index + 2, 4), 3 - index)[by]


def kernel(
    scale,
    templates,
    records,
    moveout,
    gap_start,
    gap_length,
    out,
    packed,
    unit32,
    unit_t,
    own,
    halo,
    moves,
    gaps,
    series,
    rolled,
    inverse,
    hankel,
    corr,
    lag,
    half_send,
    half_recv,
    half_own,
    x_send,
    x_recv,
    x_own,
    z_send,
    z_recv,
    local_sem,
    halo_sem,
    half_sem,
    x_sem,
    z_sem,
):
    sta = lax.axis_index("sta")
    tm = lax.axis_index("tm")
    core = lax.rem(sta, 2)
    xx = lax.rem(sta // 2, 4)
    zz = sta // 8
    zs = [paired(zz, a) for a in range(4)]
    xs = [paired(xx, b) for b in range(4)]

    def at(a, b, c):
        return {"sta": zs[a] * 8 + xs[b] * 2 + c}

    sibling = at(0, 0, 1 - core)
    barrier = pltpu.get_barrier_semaphore()

    @pl.when(tm < 7)
    def _():
        pl.semaphore_signal(
            barrier, inc=1, device_id={"tm": lax.rem(tm + 1, 8)}, device_id_type=MESH
        )

    for a, b in ((3, 0), (2, 0), (1, 0), (0, 2), (0, 1), (0, 3)):
        pl.semaphore_signal(barrier, inc=1, device_id=at(a, b, core), device_id_type=MESH)
    pl.semaphore_signal(barrier, inc=1, device_id=sibling, device_id_type=MESH)

    loads = [
        pltpu.make_async_copy(records, own, local_sem.at[0]),
        pltpu.make_async_copy(gap_start, gaps.at[0], local_sem.at[1]),
        pltpu.make_async_copy(gap_length, gaps.at[1], local_sem.at[2]),
        pltpu.make_async_copy(moveout, moves, local_sem.at[3]),
        pltpu.make_async_copy(templates, packed, local_sem.at[4]),
    ]
    for load in loads:
        load.start()

    @pl.when(tm == 7)
    def _():
        halo[...] = jnp.zeros_like(halo)

    for load in loads[:4]:
        load.wait()

    for s in range(2):
        for q in range(4):
            line = moves[s : s + 1, 128 * q : 128 * (q + 1)]
            lag[s, 128 * q : 128 * (q + 1), :] = jnp.broadcast_to(line, (128, 128)).T

    pl.semaphore_wait(barrier, 7 + jnp.where(tm > 0, 1, 0))
    halo_copy = pltpu.make_async_remote_copy(
        src_ref=own,
        dst_ref=halo,
        send_sem=halo_sem.at[0],
        recv_sem=halo_sem.at[1],
        device_id={"tm": lax.rem(tm + 7, 8)},
        device_id_type=MESH,
    )

    @pl.when(tm > 0)
    def _():
        halo_copy.start()

    loads[4].wait()

    unit32[3600:3680, :] = jnp.zeros((80, 128), jnp.float32)
    for c in range(CHANNELS):
        wide = packed[1200 * c : 1200 * (c + 1), :].astype(jnp.float32).reshape(150, 8, 128)
        norm = 1.0 / jnp.sqrt(jnp.sum(wide * wide, axis=0, keepdims=True) + 1e-06)
        unit32[1200 * c : 1200 * (c + 1), :] = (wide * norm).reshape(1200, 128)
    row = lax.broadcasted_iota(jnp.int32, (ROWS, 128), 0)
    for s in range(2):
        for q in range(4):
            parts = []
            for c in range(CHANNELS):
                taken = unit32[pl.ds(1200 * c + 2 * q + s, ROWS, stride=8), :]
                parts.append(jnp.where(row < TEMPLATE_LEN, taken, 0.0))
            parts.append(jnp.zeros((DEPTH - 3 * ROWS, 128), jnp.float32))
            block = jnp.concatenate(parts, axis=0).astype(jnp.bfloat16)
            unit_t[s, 128 * q : 128 * (q + 1), :] = block.T

    series[...] = jnp.zeros_like(series)
    for c in range(CHANNELS):
        series[2 * c : 2 * c + 2, 0:SLICE] = own[c].astype(jnp.float32)

    def spread(begin, end, base, stop):
        span = stop - base
        width = end - begin
        skip = begin - base
        line = lax.broadcasted_iota(jnp.int32, (8, span), 0)
        position = lax.broadcasted_iota(jnp.int32, (8, span), 1) + (tm * SLICE + base)
        first = jnp.zeros((8, span), jnp.int32)
        length = jnp.zeros((8, span), jnp.int32)
        for s in range(2):
            for c in range(CHANNELS):
                first = jnp.where(line == 2 * c + s, gaps[0, s, c], first)
                length = jnp.where(line == 2 * c + s, gaps[1, s, c], length)
        kept = ((position < first) | (position >= first + length)) & (position < NT)
        masked = jnp.where(kept, series[:, base:stop], 0.0)

        def ahead(value, by):
            return pltpu.roll(value, span - by, 1) if by else value

        for r in range(8):
            moved = ahead(masked, r)
            for b in range(span // 128):
                rolled[b, 8 * r : 8 * (r + 1), :] = moved[:, 128 * b : 128 * (b + 1)]
        sums = {1: masked * masked}
        for power in range(7):
            step = 1 << power
            sums[2 * step] = sums[step] + ahead(sums[step], step)
        energy = (sums[128] + ahead(sums[16], 128)) + (ahead(sums[4], 144) + ahead(sums[2], 148))
        inverse[:, begin:end] = (1.0 / jnp.sqrt(jnp.maximum(energy, 1.0)))[:, skip : skip + width]
        for s in range(2):
            hankel[s, 3 * ROWS : DEPTH, begin:end] = jnp.zeros(
                (DEPTH - 3 * ROWS, width), jnp.bfloat16
            )
            for c in range(CHANNELS):
                eight = jnp.concatenate(
                    [rolled[b, pl.ds(2 * c + s, 8, stride=8), :] for b in range(span // 128)],
                    axis=1,
                )
                weight = inverse[2 * c + s : 2 * c + s + 1, begin:end]
                for g in range(ROWS // 16):
                    pair = [
                        ahead(eight, 16 * g + 8 * h)[:, skip : skip + width] * weight
                        for h in range(2)
                    ]
                    hankel[s, ROWS * c + 16 * g : ROWS * c + 16 * (g + 1), begin:end] = (
                        jnp.concatenate(pair, axis=0).astype(jnp.bfloat16)
                    )

    def blocks(chunk):
        return [(a, b) for a in ((3, 2), (1, 0))[chunk] for b in (2, 1, 3, 0)]

    def first_row(a, b, side):
        return pl.multiple_of(128 * zs[a] + 32 * xs[b] + 16 * side, 16)

    def multiply(chunk, slot, side, begin, end):
        for s in range(2):
            rows = [unit_t[s, pl.ds(first_row(a, b, side), 16), :] for a, b in blocks(chunk)]
            corr[s, 128 * slot : 128 * (slot + 1), begin:end] = jnp.dot(
                jnp.concatenate(rows, axis=0),
                hankel[s, :, begin:end],
                preferred_element_type=jnp.float32,
            )

    lane = lax.broadcasted_iota(jnp.int32, (16, 128), 1)

    def shift(chunk, slot, side, store):
        for g, (a, b) in enumerate(blocks(chunk)):
            base = 128 * slot + 16 * g
            total = [None] * 4
            for s in range(2):
                move = lag[s, pl.ds(first_row(a, b, side), 16), :]
                near = move <= lane
                middle = move <= lane + 128
                index = (lane + move) & 127
                pieces = [corr[s, base : base + 16, 128 * j : 128 * (j + 1)] for j in range(6)]
                for j in range(4):
                    mixed = jnp.where(
                        near, pieces[j], jnp.where(middle, pieces[j + 1], pieces[j + 2])
                    )
                    moved = jnp.take_along_axis(mixed, index, axis=1, mode="promise_in_bounds")
                    total[j] = moved if s == 0 else total[j] + moved
            store(8 * chunk + g, jnp.concatenate(total, axis=1))

    def to_send(place, value):
        half_send[place] = value.astype(jnp.bfloat16)

    def to_own(place, value):
        half_own[place] = value

    def half_copy(chunk):
        return pltpu.make_async_remote_copy(
            src_ref=half_send.at[pl.ds(8 * chunk, 8)],
            dst_ref=half_recv.at[pl.ds(8 * chunk, 8)],
            send_sem=half_sem.at[0, chunk],
            recv_sem=half_sem.at[1, chunk],
            device_id=sibling,
            device_id_type=MESH,
        )

    def x_copy(chunk, b):
        return pltpu.make_async_remote_copy(
            src_ref=x_send.at[b - 1, pl.ds(2 * chunk, 2)],
            dst_ref=x_recv.at[b - 1, pl.ds(2 * chunk, 2)],
            send_sem=x_sem.at[0, chunk, b - 1],
            recv_sem=x_sem.at[1, chunk, b - 1],
            device_id=at(0, b, core),
            device_id_type=MESH,
        )

    def z_copy(a):
        return pltpu.make_async_remote_copy(
            src_ref=z_send.at[a - 1],
            dst_ref=z_recv.at[a - 1],
            send_sem=z_sem.at[0, a - 1],
            recv_sem=z_sem.at[1, a - 1],
            device_id=at(a, 0, core),
            device_id_type=MESH,
        )

    stages = [(0, 0, 1 - core), (1, 1, 1 - core), (0, 2, core), (1, 3, core)]
    spread(0, NEAR, 0, SLICE)
    for chunk, slot, side in stages:
        multiply(chunk, slot, side, 0, NEAR)

    @pl.when(tm > 0)
    def _():
        halo_copy.wait_send()

    @pl.when(tm < 7)
    def _():
        halo_copy.wait_recv()

    for c in range(CHANNELS):
        series[2 * c : 2 * c + 2, SLICE:WIDE] = halo[c].astype(jnp.float32)
    spread(NEAR, FULL, NEAR, WIDE)

    for chunk, slot, side in stages:
        multiply(chunk, slot, side, NEAR, FULL)
        shift(chunk, slot, side, to_send if slot < 2 else to_own)
        if slot < 2:
            half_copy(chunk).start()

    def pair_sum(chunk, i, b):
        place = 8 * chunk + 4 * i + (2, 1, 3, 0).index(b)
        return half_own[place] + half_recv[place].astype(jnp.float32)

    for chunk in range(2):
        half_copy(chunk).wait()
        for b in (2, 1, 3):
            for i in range(2):
                x_send[b - 1, 2 * chunk + i] = pair_sum(chunk, i, b).astype(jnp.bfloat16)
            x_copy(chunk, b).start()
        for i in range(2):
            x_own[2 * chunk + i] = pair_sum(chunk, i, 0)
    for chunk in range(2):
        for b in (1, 3, 2):
            x_copy(chunk, b).wait()
        for i in range(2):
            total = x_own[2 * chunk + i]
            for b in range(3):
                total = total + x_recv[b, 2 * chunk + i].astype(jnp.float32)
            a = 3 - 2 * chunk - i
            if a:
                z_send[a - 1] = total.astype(jnp.bfloat16)
                z_copy(a).start()
    for a in (3, 2, 1):
        z_copy(a).wait()
        total = total + z_recv[a - 1].astype(jnp.float32)
    out[...] = total * scale


def shards(records, templates, moveout, gap_start, gap_length):
    stations = records.shape[0] * lax.axis_size("sta")
    scale = math.sqrt(TEMPLATE_LEN / (3.0 * stations))
    lines = jnp.transpose(templates, (2, 3, 1, 0)).reshape(450, 2, 4, 128)
    lines = jnp.transpose(lines, (0, 2, 1, 3)).reshape(3600, 128)
    whole = pl.BlockSpec(memory_space=pltpu.HBM)
    return pl.pallas_call(
        functools.partial(kernel, scale),
        out_shape=jax.ShapeDtypeStruct((16, SLICE), jnp.float32),
        in_specs=[whole] * 5,
        out_specs=pl.BlockSpec(memory_space=pltpu.VMEM),
        scratch_shapes=[
            pltpu.VMEM((3600, 128), jnp.bfloat16),
            pltpu.VMEM((3680, 128), jnp.float32),
            pltpu.VMEM((2, TEMPLATES, DEPTH), jnp.bfloat16),
            pltpu.VMEM((3, 2, SLICE), jnp.bfloat16),
            pltpu.VMEM((3, 2, SLICE), jnp.bfloat16),
            pltpu.VMEM((2, TEMPLATES), jnp.int32),
            pltpu.SMEM((2, 2, 3), jnp.int32),
            pltpu.VMEM((8, WIDE), jnp.float32),
            pltpu.VMEM((8, 64, 128), jnp.float32),
            pltpu.VMEM((8, FULL), jnp.float32),
            pltpu.VMEM((2, DEPTH, FULL), jnp.bfloat16),
            pltpu.VMEM((2, TEMPLATES, FULL), jnp.float32),
            pltpu.VMEM((2, TEMPLATES, 128), jnp.int32),
            pltpu.VMEM((16, 16, SLICE), jnp.bfloat16),
            pltpu.VMEM((16, 16, SLICE), jnp.bfloat16),
            pltpu.VMEM((16, 16, SLICE), jnp.float32),
            pltpu.VMEM((3, 4, 16, SLICE), jnp.bfloat16),
            pltpu.VMEM((3, 4, 16, SLICE), jnp.bfloat16),
            pltpu.VMEM((4, 16, SLICE), jnp.float32),
            pltpu.VMEM((3, 16, SLICE), jnp.bfloat16),
            pltpu.VMEM((3, 16, SLICE), jnp.bfloat16),
            pltpu.SemaphoreType.DMA((5,)),
            pltpu.SemaphoreType.DMA((2,)),
            pltpu.SemaphoreType.DMA((2, 2)),
            pltpu.SemaphoreType.DMA((2, 2, 3)),
            pltpu.SemaphoreType.DMA((2, 3)),
        ],
        compiler_params=pltpu.CompilerParams(
            collective_id=0, has_side_effects=True, vmem_limit_bytes=40 * 1024 * 1024
        ),
    )(
        *[
            pltpu.with_memory_space_constraint(value, pltpu.HBM)
            for value in (
                lines,
                jnp.transpose(records, (1, 0, 2)),
                jnp.transpose(moveout, (1, 0)),
                gap_start,
                gap_length,
            )
        ]
    )


def solution(mesh):
    placed = (
        P("sta", None, "tm"),
        P(None, "sta", None, None),
        P(None, "sta"),
        P("sta", None),
        P("sta", None),
    )
    return jax.shard_map(
        shards, mesh=mesh, in_specs=placed, out_specs=P("sta", "tm"), check_vma=False
    )
```

```python
import functools
import math

import jax
import jax.numpy as jnp
from jax import lax
from jax.experimental import pallas as pl
from jax.experimental.pallas import tpu as pltpu
from jax.sharding import PartitionSpec as P

CHANNELS = 3
TEMPLATE_LEN = 150
TEMPLATES = 512
MAXMO = 256
NT = 4096
SLICE = 512
WIDE = 1024
FULL = SLICE + MAXMO
NEAR = 256
ROWS = 160
DEPTH = 512
MESH = pl.DeviceIdType.MESH


def paired(index, by):
    return (index, index + 1 - 2 * lax.rem(index, 2), lax.rem(index + 2, 4), 3 - index)[by]


def kernel(
    scale,
    templates,
    records,
    moveout,
    gap_start,
    gap_length,
    out,
    packed,
    unit32,
    unit_t,
    unit_in,
    own,
    moves,
    gaps,
    line_send,
    line_in,
    halo,
    series,
    rolled,
    inverse,
    hankel,
    corr,
    lag,
    x_send,
    x_recv,
    x_own,
    z_send,
    z_recv,
    local_sem,
    halo_sem,
    pair_sem,
    x_sem,
    z_sem,
):
    sta = lax.axis_index("sta")
    tm = lax.axis_index("tm")
    core = lax.rem(sta, 2)
    xx = lax.rem(sta // 2, 4)
    zz = sta // 8
    zs = [paired(zz, a) for a in range(4)]
    xs = [paired(xx, b) for b in range(4)]

    def at(a, b, c):
        return {"sta": zs[a] * 8 + xs[b] * 2 + c}

    sibling = at(0, 0, 1 - core)
    barrier = pltpu.get_barrier_semaphore()

    @pl.when(tm < 7)
    def _():
        for c in range(2):
            pl.semaphore_signal(
                barrier,
                inc=1,
                device_id={**at(0, 0, c), "tm": lax.rem(tm + 1, 8)},
                device_id_type=MESH,
            )

    for a, b in ((3, 0), (2, 0), (1, 0), (0, 2), (0, 1), (0, 3)):
        pl.semaphore_signal(barrier, inc=1, device_id=at(a, b, core), device_id_type=MESH)
    pl.semaphore_signal(barrier, inc=1, device_id=sibling, device_id_type=MESH)

    loads = [
        pltpu.make_async_copy(records, own, local_sem.at[0]),
        pltpu.make_async_copy(gap_start, gaps.at[0], local_sem.at[1]),
        pltpu.make_async_copy(gap_length, gaps.at[1], local_sem.at[2]),
        pltpu.make_async_copy(moveout, moves.at[0], local_sem.at[3]),
        pltpu.make_async_copy(templates, packed, local_sem.at[4]),
    ]
    for load in loads:
        load.start()

    @pl.when(tm == 7)
    def _():
        halo[...] = jnp.zeros_like(halo)

    for load in loads[:4]:
        load.wait()

    series[...] = jnp.zeros_like(series)
    for c in range(CHANNELS):
        series[0, 2 * c : 2 * c + 2, 0:SLICE] = own[c].astype(jnp.float32)
    line = lax.broadcasted_iota(jnp.int32, (8, SLICE), 0)
    position = lax.broadcasted_iota(jnp.int32, (8, SLICE), 1) + tm * SLICE
    first = jnp.zeros((8, SLICE), jnp.int32)
    length = jnp.zeros((8, SLICE), jnp.int32)
    for s in range(2):
        for c in range(CHANNELS):
            first = jnp.where(line == 2 * c + s, gaps[0, s, c], first)
            length = jnp.where(line == 2 * c + s, gaps[1, s, c], length)
    kept = ((position < first) | (position >= first + length)) & (position < NT)
    masked = jnp.where(kept, series[0, :, 0:SLICE], 0.0)
    series[0, :, 0:SLICE] = masked
    line_send[...] = jnp.concatenate(
        [masked[:, : SLICE // 2], masked[:, SLICE // 2 :]], axis=0
    ).astype(jnp.bfloat16)

    def unfold(value):
        wide = value.astype(jnp.float32)
        return jnp.concatenate([wide[:8], wide[8:]], axis=1)

    def halo_copy(other):
        to = 1 - core if other else core
        return pltpu.make_async_remote_copy(
            src_ref=line_send,
            dst_ref=halo.at[other],
            send_sem=halo_sem.at[0, other],
            recv_sem=halo_sem.at[1, other],
            device_id={**at(0, 0, to), "tm": lax.rem(tm + 7, 8)},
            device_id_type=MESH,
        )

    def to_sibling(source, target, index):
        return pltpu.make_async_remote_copy(
            src_ref=source,
            dst_ref=target,
            send_sem=pair_sem.at[0, index],
            recv_sem=pair_sem.at[1, index],
            device_id=sibling,
            device_id_type=MESH,
        )

    line_copy = to_sibling(line_send, line_in, 0)
    move_copy = to_sibling(moves.at[0], moves.at[1], 1)
    unit_copy = to_sibling(unit_t.at[:, :, 1 - core], unit_in, 2)

    pl.semaphore_wait(barrier, 7 + jnp.where(tm > 0, 2, 0))

    @pl.when(tm > 0)
    def _():
        halo_copy(0).start()
        halo_copy(1).start()

    line_copy.start()
    move_copy.start()

    def spread_moves(side):
        for s in range(2):
            for q in range(4):
                line = moves[side, s : s + 1, 128 * q : 128 * (q + 1)]
                lag[2 * side + s, 128 * q : 128 * (q + 1), :] = jnp.broadcast_to(line, (128, 128)).T

    spread_moves(0)
    loads[4].wait()

    unit32[3600:3680, :] = jnp.zeros((80, 128), jnp.float32)
    for c in range(CHANNELS):
        wide = packed[1200 * c : 1200 * (c + 1), :].astype(jnp.float32).reshape(150, 8, 128)
        norm = 1.0 / jnp.sqrt(jnp.sum(wide * wide, axis=0, keepdims=True) + 1e-06)
        unit32[1200 * c : 1200 * (c + 1), :] = (wide * norm).reshape(1200, 128)
    row = lax.broadcasted_iota(jnp.int32, (ROWS, 128), 0)
    for s in range(2):
        for q in range(4):
            parts = []
            for c in range(CHANNELS):
                taken = unit32[pl.ds(1200 * c + 2 * q + s, ROWS, stride=8), :]
                parts.append(jnp.where(row < TEMPLATE_LEN, taken, 0.0))
            parts.append(jnp.zeros((DEPTH - 3 * ROWS, 128), jnp.float32))
            block = jnp.concatenate(parts, axis=0).astype(jnp.bfloat16)
            unit_t[s, 4 * q : 4 * (q + 1)] = block.T.reshape(4, 2, 16, DEPTH)
    unit_copy.start()

    def spread(side, begin, end, base, stop):
        span = stop - base
        width = end - begin
        skip = begin - base
        masked = series[side, :, base:stop]

        def ahead(value, by):
            return pltpu.roll(value, span - by, 1) if by else value

        eights = [ahead(masked, r) for r in range(8)]
        for r in range(8):
            for b in range(span // 128):
                rolled[side, b, 8 * r : 8 * (r + 1), :] = eights[r][:, 128 * b : 128 * (b + 1)]

        def tree(values):
            while len(values) > 1:
                values = [sum(values[i + 1 : i + 2], values[i]) for i in range(0, len(values), 2)]
            return values[0]

        squares = [value * value for value in eights]
        six = tree(squares[:6])
        eight_sum = six + (squares[6] + squares[7])
        most = tree([ahead(eight_sum, 8 * i) for i in range(8)])
        rest = tree([ahead(eight_sum, 128), ahead(eight_sum, 136), ahead(six, 144)])
        energy = (most + ahead(most, 64)) + rest
        inverse[side, :, begin:end] = (1.0 / jnp.sqrt(jnp.maximum(energy, 1.0)))[:, skip : skip + width]
        for s in range(2):
            hankel[2 * side + s, 3 * ROWS : DEPTH, begin:end] = jnp.zeros(
                (DEPTH - 3 * ROWS, width), jnp.bfloat16
            )
            for c in range(CHANNELS):
                eight = jnp.concatenate(
                    [rolled[side, b, pl.ds(2 * c + s, 8, stride=8), :] for b in range(span // 128)],
                    axis=1,
                )
                weight = inverse[side, 2 * c + s : 2 * c + s + 1, begin:end]
                for g in range(ROWS // 16):
                    pair = [
                        ahead(eight, 16 * g + 8 * h)[:, skip : skip + width] * weight
                        for h in range(2)
                    ]
                    hankel[
                        2 * side + s, ROWS * c + 16 * g : ROWS * c + 16 * (g + 1), begin:end
                    ] = (
                        jnp.concatenate(pair, axis=0).astype(jnp.bfloat16)
                    )

    def blocks(chunk):
        return [(a, b) for a in ((3, 2), (1, 0))[chunk] for b in (2, 1, 3, 0)]

    def multiply(side, chunk, begin, end):
        for s in range(2):
            rows = []
            for a, b in blocks(chunk):
                block = 4 * zs[a] + xs[b]
                rows.append(unit_in[s, block] if side else unit_t[s, block, core])
            corr[2 * side + s, 128 * chunk : 128 * (chunk + 1), begin:end] = jnp.dot(
                jnp.concatenate(rows, axis=0),
                hankel[2 * side + s, :, begin:end],
                preferred_element_type=jnp.float32,
            )

    lane = lax.broadcasted_iota(jnp.int32, (16, 128), 1)

    def shift(chunk):
        for g, (a, b) in enumerate(blocks(chunk)):
            base = 128 * chunk + 16 * g
            start = pl.multiple_of(128 * zs[a] + 32 * xs[b] + 16 * core, 16)
            total = [None] * 4
            for s in range(4):
                move = lag[s, pl.ds(start, 16), :]
                near = move <= lane
                middle = move <= lane + 128
                index = (lane + move) & 127
                pieces = [corr[s, base : base + 16, 128 * j : 128 * (j + 1)] for j in range(6)]
                for j in range(4):
                    mixed = jnp.where(
                        near, pieces[j], jnp.where(middle, pieces[j + 1], pieces[j + 2])
                    )
                    moved = jnp.take_along_axis(mixed, index, axis=1, mode="promise_in_bounds")
                    total[j] = moved if s == 0 else total[j] + moved
            value = jnp.concatenate(total, axis=1)
            if b:
                x_send[b - 1, 3 - a] = value.astype(jnp.bfloat16)
            else:
                x_own[3 - a] = value

    def x_copy(chunk, b):
        return pltpu.make_async_remote_copy(
            src_ref=x_send.at[b - 1, pl.ds(2 * chunk, 2)],
            dst_ref=x_recv.at[b - 1, pl.ds(2 * chunk, 2)],
            send_sem=x_sem.at[0, chunk, b - 1],
            recv_sem=x_sem.at[1, chunk, b - 1],
            device_id=at(0, b, core),
            device_id_type=MESH,
        )

    def z_copy(a):
        return pltpu.make_async_remote_copy(
            src_ref=z_send.at[a - 1],
            dst_ref=z_recv.at[a - 1],
            send_sem=z_sem.at[0, a - 1],
            recv_sem=z_sem.at[1, a - 1],
            device_id=at(a, 0, core),
            device_id_type=MESH,
        )

    spread(0, 0, NEAR, 0, SLICE)
    for chunk in range(2):
        multiply(0, chunk, 0, NEAR)
    line_copy.wait()
    move_copy.wait()
    series[1, :, 0:SLICE] = unfold(line_in[...])
    spread_moves(1)
    spread(1, 0, NEAR, 0, SLICE)
    unit_copy.wait()
    for chunk in range(2):
        multiply(1, chunk, 0, NEAR)

    @pl.when(tm > 0)
    def _():
        for other in range(2):
            halo_copy(other).wait_send()

    @pl.when(tm < 7)
    def _():
        for other in (1, 0):
            halo_copy(other).wait_recv()

    for side in range(2):
        series[side, :, SLICE:WIDE] = unfold(halo[side])
        spread(side, NEAR, FULL, NEAR, WIDE)
    for chunk in range(2):
        for side in range(2):
            multiply(side, chunk, NEAR, FULL)
        shift(chunk)
        for b in (2, 1, 3):
            x_copy(chunk, b).start()
    for chunk in range(2):
        for b in (1, 3, 2):
            x_copy(chunk, b).wait()
        for i in range(2):
            total = x_own[2 * chunk + i]
            for b in range(3):
                total = total + x_recv[b, 2 * chunk + i].astype(jnp.float32)
            a = 3 - 2 * chunk - i
            if a:
                z_send[a - 1] = total.astype(jnp.bfloat16)
                z_copy(a).start()
    for a in (3, 2, 1):
        z_copy(a).wait()
        total = total + z_recv[a - 1].astype(jnp.float32)
    out[...] = total * scale


def shards(records, templates, moveout, gap_start, gap_length):
    stations = records.shape[0] * lax.axis_size("sta")
    scale = math.sqrt(TEMPLATE_LEN / (3.0 * stations))
    lines = jnp.transpose(templates, (2, 3, 1, 0)).reshape(450, 2, 4, 128)
    lines = jnp.transpose(lines, (0, 2, 1, 3)).reshape(3600, 128)
    whole = pl.BlockSpec(memory_space=pltpu.HBM)
    return pl.pallas_call(
        functools.partial(kernel, scale),
        out_shape=jax.ShapeDtypeStruct((16, SLICE), jnp.float32),
        in_specs=[whole] * 5,
        out_specs=pl.BlockSpec(memory_space=pltpu.VMEM),
        scratch_shapes=[
            pltpu.VMEM((3600, 128), jnp.bfloat16),
            pltpu.VMEM((3680, 128), jnp.float32),
            pltpu.VMEM((2, 16, 2, 16, DEPTH), jnp.bfloat16),
            pltpu.VMEM((2, 16, 16, DEPTH), jnp.bfloat16),
            pltpu.VMEM((3, 2, SLICE), jnp.bfloat16),
            pltpu.VMEM((2, 2, TEMPLATES), jnp.int32),
            pltpu.SMEM((2, 2, 3), jnp.int32),
            pltpu.VMEM((16, SLICE // 2), jnp.bfloat16),
            pltpu.VMEM((16, SLICE // 2), jnp.bfloat16),
            pltpu.VMEM((2, 16, SLICE // 2), jnp.bfloat16),
            pltpu.VMEM((2, 8, WIDE), jnp.float32),
            pltpu.VMEM((2, 8, 64, 128), jnp.float32),
            pltpu.VMEM((2, 8, FULL), jnp.float32),
            pltpu.VMEM((4, DEPTH, FULL), jnp.bfloat16),
            pltpu.VMEM((4, TEMPLATES // 2, FULL), jnp.float32),
            pltpu.VMEM((4, TEMPLATES, 128), jnp.int32),
            pltpu.VMEM((3, 4, 16, SLICE), jnp.bfloat16),
            pltpu.VMEM((3, 4, 16, SLICE), jnp.bfloat16),
            pltpu.VMEM((4, 16, SLICE), jnp.float32),
            pltpu.VMEM((3, 16, SLICE), jnp.bfloat16),
            pltpu.VMEM((3, 16, SLICE), jnp.bfloat16),
            pltpu.SemaphoreType.DMA((5,)),
            pltpu.SemaphoreType.DMA((2, 2)),
            pltpu.SemaphoreType.DMA((2, 3)),
            pltpu.SemaphoreType.DMA((2, 2, 3)),
            pltpu.SemaphoreType.DMA((2, 3)),
        ],
        compiler_params=pltpu.CompilerParams(
            collective_id=0, has_side_effects=True, vmem_limit_bytes=40 * 1024 * 1024
        ),
    )(
        *[
            pltpu.with_memory_space_constraint(value, pltpu.HBM)
            for value in (
                lines,
                jnp.transpose(records, (1, 0, 2)),
                jnp.transpose(moveout, (1, 0)),
                gap_start,
                gap_length,
            )
        ]
    )


def solution(mesh):
    placed = (
        P("sta", None, "tm"),
        P(None, "sta", None, None),
        P(None, "sta"),
        P("sta", None),
        P("sta", None),
    )
    return jax.shard_map(
        shards, mesh=mesh, in_specs=placed, out_specs=P("sta", "tm"), check_vma=False
    )
```

```python
import functools
import math

import jax
import jax.numpy as jnp
from jax import lax
from jax.experimental import pallas as pl
from jax.experimental.pallas import tpu as pltpu
from jax.sharding import PartitionSpec as P

CHANNELS = 3
TEMPLATE_LEN = 150
TEMPLATES = 512
MAXMO = 256
NT = 4096
SLICE = 512
WIDE = 1024
FULL = SLICE + MAXMO
NEAR = 256
ROWS = 160
DEPTH = 512
MESH = pl.DeviceIdType.MESH


def paired(index, by):
    return (index, index + 1 - 2 * lax.rem(index, 2), lax.rem(index + 2, 4), 3 - index)[by]


def kernel(
    scale,
    templates,
    records,
    moveout,
    gap_start,
    gap_length,
    out,
    packed,
    unit32,
    unit_t,
    unit_in,
    own,
    moves,
    gaps,
    lines,
    halo,
    series,
    rolled,
    inverse,
    hankel,
    corr,
    lag,
    x_send,
    x_recv,
    x_own,
    z_send,
    z_recv,
    local_sem,
    halo_sem,
    pair_sem,
    x_sem,
    z_sem,
):
    sta = lax.axis_index("sta")
    tm = lax.axis_index("tm")
    core = lax.rem(sta, 2)
    xx = lax.rem(sta // 2, 4)
    zz = sta // 8
    zs = [paired(zz, a) for a in range(4)]
    xs = [paired(xx, b) for b in range(4)]

    def at(a, b, c):
        return {"sta": zs[a] * 8 + xs[b] * 2 + c}

    sibling = at(0, 0, 1 - core)
    barrier = pltpu.get_barrier_semaphore()

    through = core == 1

    @pl.when(through & (tm < 7))
    def _():
        pl.semaphore_signal(
            barrier, inc=1, device_id={"tm": lax.rem(tm + 1, 8)}, device_id_type=MESH
        )

    for a, b in ((3, 0), (2, 0), (1, 0), (0, 2), (0, 1), (0, 3)):
        pl.semaphore_signal(barrier, inc=1, device_id=at(a, b, core), device_id_type=MESH)
    pl.semaphore_signal(barrier, inc=1, device_id=sibling, device_id_type=MESH)

    loads = [
        pltpu.make_async_copy(records, own, local_sem.at[0]),
        pltpu.make_async_copy(gap_start, gaps.at[0], local_sem.at[1]),
        pltpu.make_async_copy(gap_length, gaps.at[1], local_sem.at[2]),
        pltpu.make_async_copy(moveout, moves.at[0], local_sem.at[3]),
        pltpu.make_async_copy(templates, packed, local_sem.at[4]),
    ]
    for load in loads:
        load.start()

    @pl.when(tm == 7)
    def _():
        halo[...] = jnp.zeros_like(halo)

    for load in loads[:4]:
        load.wait()

    series[...] = jnp.zeros_like(series)
    for c in range(CHANNELS):
        series[2 * c : 2 * c + 2, 0:SLICE] = own[c].astype(jnp.float32)
    line = lax.broadcasted_iota(jnp.int32, (8, SLICE), 0)
    position = lax.broadcasted_iota(jnp.int32, (8, SLICE), 1) + tm * SLICE
    first = jnp.zeros((8, SLICE), jnp.int32)
    length = jnp.zeros((8, SLICE), jnp.int32)
    for s in range(2):
        for c in range(CHANNELS):
            first = jnp.where(line == 2 * c + s, gaps[0, s, c], first)
            length = jnp.where(line == 2 * c + s, gaps[1, s, c], length)
    kept = ((position < first) | (position >= first + length)) & (position < NT)
    masked = jnp.where(kept, series[0:8, 0:SLICE], 0.0)
    series[0:8, 0:SLICE] = masked
    lines[core] = jnp.concatenate(
        [masked[:, : SLICE // 2], masked[:, SLICE // 2 :]], axis=0
    ).astype(jnp.bfloat16)

    def unfold(value):
        wide = value.astype(jnp.float32)
        return jnp.concatenate([wide[:8], wide[8:]], axis=1)

    halo_copy = pltpu.make_async_remote_copy(
        src_ref=lines,
        dst_ref=halo,
        send_sem=halo_sem.at[0],
        recv_sem=halo_sem.at[1],
        device_id={"tm": lax.rem(tm + 7, 8)},
        device_id_type=MESH,
    )

    def to_sibling(source, target, index):
        return pltpu.make_async_remote_copy(
            src_ref=source,
            dst_ref=target,
            send_sem=pair_sem.at[0, index],
            recv_sem=pair_sem.at[1, index],
            device_id=sibling,
            device_id_type=MESH,
        )

    line_copy = to_sibling(lines.at[core], lines.at[core], 0)
    move_copy = to_sibling(moves.at[0], moves.at[1], 1)
    unit_copy = to_sibling(unit_t.at[:, :, 1 - core], unit_in, 2)

    hand_on = to_sibling(halo, halo, 3)
    sends = through & (tm > 0)
    pl.semaphore_wait(barrier, 7 + jnp.where(sends, 1, 0))
    line_copy.start()

    @pl.when(sends)
    def _():
        line_copy.wait_recv()
        halo_copy.start()

    move_copy.start()

    def spread_moves(side):
        for s in range(2):
            for q in range(4):
                line = moves[side, s : s + 1, 128 * q : 128 * (q + 1)]
                lag[2 * side + s, 128 * q : 128 * (q + 1), :] = jnp.broadcast_to(line, (128, 128)).T

    spread_moves(0)
    loads[4].wait()

    unit32[3600:3680, :] = jnp.zeros((80, 128), jnp.float32)
    for c in range(CHANNELS):
        wide = packed[1200 * c : 1200 * (c + 1), :].astype(jnp.float32).reshape(150, 8, 128)
        norm = 1.0 / jnp.sqrt(jnp.sum(wide * wide, axis=0, keepdims=True) + 1e-06)
        unit32[1200 * c : 1200 * (c + 1), :] = (wide * norm).reshape(1200, 128)
    row = lax.broadcasted_iota(jnp.int32, (ROWS, 128), 0)
    for s in range(2):
        for q in range(4):
            parts = []
            for c in range(CHANNELS):
                taken = unit32[pl.ds(1200 * c + 2 * q + s, ROWS, stride=8), :]
                parts.append(jnp.where(row < TEMPLATE_LEN, taken, 0.0))
            parts.append(jnp.zeros((DEPTH - 3 * ROWS, 128), jnp.float32))
            block = jnp.concatenate(parts, axis=0).astype(jnp.bfloat16)
            unit_t[s, 4 * q : 4 * (q + 1)] = block.T.reshape(4, 2, 16, DEPTH)
    unit_copy.start()

    def spread(begin, end, base, stop):
        span = stop - base
        width = end - begin
        skip = begin - base
        masked = series[:, base:stop].astype(jnp.bfloat16)

        def ahead(value, by):
            return pltpu.roll(value, span - by, 1) if by else value

        rows = [ahead(masked, r).astype(jnp.float32) for r in range(16)]
        for r in range(16):
            for b in range(span // 128):
                rolled[b, 16 * r : 16 * (r + 1), :] = rows[r][:, 128 * b : 128 * (b + 1)]
        squares = [value * value for value in rows[:8]]
        six = ((squares[0] + squares[1]) + (squares[2] + squares[3])) + (squares[4] + squares[5])
        over8 = six + (squares[6] + squares[7])
        over16 = over8 + ahead(over8, 8)
        over32 = over16 + (ahead(over8, 16) + ahead(over8, 24))
        over128 = (over32 + ahead(over32, 32)) + (ahead(over32, 64) + ahead(over32, 96))
        energy = over128 + (ahead(over16, 128) + ahead(six, 144))
        inverse[:, begin:end] = (1.0 / jnp.sqrt(jnp.maximum(energy, 1.0)))[:, skip : skip + width]
        for s in range(4):
            hankel[s, 3 * ROWS : DEPTH, begin:end] = jnp.zeros(
                (DEPTH - 3 * ROWS, width), jnp.bfloat16
            )
            for c in range(CHANNELS):
                line = 8 * (s // 2) + 2 * c + s % 2
                sixteen = jnp.concatenate(
                    [rolled[b, pl.ds(line, 16, stride=16), :] for b in range(span // 128)],
                    axis=1,
                ).astype(jnp.bfloat16)
                weight = inverse[line : line + 1, begin:end]
                for b in range(8):
                    moved = ahead(sixteen, 16 * b)
                    for h in range(2 if b < 2 else 1):
                        top = ROWS * c + 16 * b + 128 * h
                        taken = moved[:, skip + 128 * h : skip + 128 * h + width]
                        hankel[s, top : top + 16, begin:end] = (
                            taken.astype(jnp.float32) * weight
                        ).astype(jnp.bfloat16)

    def blocks(chunk):
        return [(a, b) for a in ((3, 2), (1, 0))[chunk] for b in (2, 1, 3, 0)]

    def multiply(side, chunk, begin, end):
        for s in range(2):
            rows = []
            for a, b in blocks(chunk):
                block = 4 * zs[a] + xs[b]
                rows.append(unit_in[s, block] if side else unit_t[s, block, core])
            corr[2 * side + s, 128 * chunk : 128 * (chunk + 1), begin:end] = jnp.dot(
                jnp.concatenate(rows, axis=0),
                hankel[2 * side + s, :, begin:end],
                preferred_element_type=jnp.float32,
            )

    lane = lax.broadcasted_iota(jnp.int32, (16, 128), 1)

    def shift(chunk):
        for g, (a, b) in enumerate(blocks(chunk)):
            base = 128 * chunk + 16 * g
            start = pl.multiple_of(128 * zs[a] + 32 * xs[b] + 16 * core, 16)
            total = [None] * 4
            for s in range(4):
                move = lag[s, pl.ds(start, 16), :]
                near = move <= lane
                middle = move <= lane + 128
                index = (lane + move) & 127
                pieces = [corr[s, base : base + 16, 128 * j : 128 * (j + 1)] for j in range(6)]
                for j in range(4):
                    mixed = jnp.where(
                        near, pieces[j], jnp.where(middle, pieces[j + 1], pieces[j + 2])
                    )
                    moved = jnp.take_along_axis(mixed, index, axis=1, mode="promise_in_bounds")
                    total[j] = moved if s == 0 else total[j] + moved
            value = jnp.concatenate(total, axis=1)
            if b:
                x_send[b - 1, 3 - a] = value.astype(jnp.bfloat16)
            else:
                x_own[3 - a] = value

    def x_copy(chunk, b):
        return pltpu.make_async_remote_copy(
            src_ref=x_send.at[b - 1, pl.ds(2 * chunk, 2)],
            dst_ref=x_recv.at[b - 1, pl.ds(2 * chunk, 2)],
            send_sem=x_sem.at[0, chunk, b - 1],
            recv_sem=x_sem.at[1, chunk, b - 1],
            device_id=at(0, b, core),
            device_id_type=MESH,
        )

    def z_copy(a):
        return pltpu.make_async_remote_copy(
            src_ref=z_send.at[a - 1],
            dst_ref=z_recv.at[a - 1],
            send_sem=z_sem.at[0, a - 1],
            recv_sem=z_sem.at[1, a - 1],
            device_id=at(a, 0, core),
            device_id_type=MESH,
        )

    @pl.when(jnp.logical_not(sends))
    def _():
        line_copy.wait_recv()

    line_copy.wait_send()
    move_copy.wait()
    series[8:16, 0:SLICE] = unfold(lines[1 - core])
    spread_moves(1)
    spread(0, NEAR, 0, SLICE)
    for chunk in range(2):
        multiply(0, chunk, 0, NEAR)
    unit_copy.wait()
    for chunk in range(2):
        multiply(1, chunk, 0, NEAR)

    @pl.when(sends)
    def _():
        halo_copy.wait_send()

    @pl.when(through & (tm < 7))
    def _():
        halo_copy.wait_recv()
        hand_on.start()

    @pl.when((core == 0) & (tm < 7))
    def _():
        hand_on.wait_recv()

    series[0:8, SLICE:WIDE] = unfold(halo[core])
    series[8:16, SLICE:WIDE] = unfold(halo[1 - core])
    spread(NEAR, FULL, NEAR, WIDE)
    for chunk in range(2):
        for side in range(2):
            multiply(side, chunk, NEAR, FULL)
        shift(chunk)
        for b in (2, 1, 3):
            x_copy(chunk, b).start()
    for chunk in range(2):
        for b in (1, 3, 2):
            x_copy(chunk, b).wait()
        for i in range(2):
            total = x_own[2 * chunk + i]
            for b in range(3):
                total = total + x_recv[b, 2 * chunk + i].astype(jnp.float32)
            a = 3 - 2 * chunk - i
            if a:
                z_send[a - 1] = total.astype(jnp.bfloat16)
                z_copy(a).start()
    for a in (3, 2, 1):
        z_copy(a).wait()
        total = total + z_recv[a - 1].astype(jnp.float32)
    out[...] = total * scale

    @pl.when(through & (tm < 7))
    def _():
        hand_on.wait_send()


def shards(records, templates, moveout, gap_start, gap_length):
    stations = records.shape[0] * lax.axis_size("sta")
    scale = math.sqrt(TEMPLATE_LEN / (3.0 * stations))
    lines = jnp.transpose(templates, (2, 3, 1, 0)).reshape(450, 2, 4, 128)
    lines = jnp.transpose(lines, (0, 2, 1, 3)).reshape(3600, 128)
    whole = pl.BlockSpec(memory_space=pltpu.HBM)
    return pl.pallas_call(
        functools.partial(kernel, scale),
        out_shape=jax.ShapeDtypeStruct((16, SLICE), jnp.float32),
        in_specs=[whole] * 5,
        out_specs=pl.BlockSpec(memory_space=pltpu.VMEM),
        scratch_shapes=[
            pltpu.VMEM((3600, 128), jnp.bfloat16),
            pltpu.VMEM((3680, 128), jnp.float32),
            pltpu.VMEM((2, 16, 2, 16, DEPTH), jnp.bfloat16),
            pltpu.VMEM((2, 16, 16, DEPTH), jnp.bfloat16),
            pltpu.VMEM((3, 2, SLICE), jnp.bfloat16),
            pltpu.VMEM((2, 2, TEMPLATES), jnp.int32),
            pltpu.SMEM((2, 2, 3), jnp.int32),
            pltpu.VMEM((2, 16, SLICE // 2), jnp.bfloat16),
            pltpu.VMEM((2, 16, SLICE // 2), jnp.bfloat16),
            pltpu.VMEM((16, WIDE), jnp.float32),
            pltpu.VMEM((8, 256, 128), jnp.float32),
            pltpu.VMEM((16, FULL), jnp.float32),
            pltpu.VMEM((4, DEPTH, FULL), jnp.bfloat16),
            pltpu.VMEM((4, TEMPLATES // 2, FULL), jnp.float32),
            pltpu.VMEM((4, TEMPLATES, 128), jnp.int32),
            pltpu.VMEM((3, 4, 16, SLICE), jnp.bfloat16),
            pltpu.VMEM((3, 4, 16, SLICE), jnp.bfloat16),
            pltpu.VMEM((4, 16, SLICE), jnp.float32),
            pltpu.VMEM((3, 16, SLICE), jnp.bfloat16),
            pltpu.VMEM((3, 16, SLICE), jnp.bfloat16),
            pltpu.SemaphoreType.DMA((5,)),
            pltpu.SemaphoreType.DMA((2,)),
            pltpu.SemaphoreType.DMA((2, 4)),
            pltpu.SemaphoreType.DMA((2, 2, 3)),
            pltpu.SemaphoreType.DMA((2, 3)),
        ],
        compiler_params=pltpu.CompilerParams(
            collective_id=0, has_side_effects=True, vmem_limit_bytes=40 * 1024 * 1024
        ),
    )(
        *[
            pltpu.with_memory_space_constraint(value, pltpu.HBM)
            for value in (
                lines,
                jnp.transpose(records, (1, 0, 2)),
                jnp.transpose(moveout, (1, 0)),
                gap_start,
                gap_length,
            )
        ]
    )


def solution(mesh):
    placed = (
        P("sta", None, "tm"),
        P(None, "sta", None, None),
        P(None, "sta"),
        P("sta", None),
        P("sta", None),
    )
    return jax.shard_map(
        shards, mesh=mesh, in_specs=placed, out_specs=P("sta", "tm"), check_vma=False
    )
```
